32 devices in a mesh: shot: 2 (over x), dom: 8 (over z, y), sub: 2 (over core).
Axes of the slice: x: 2, y: 2, z: 4, core: 2. Of those that a mesh axis runs over, the one named last changes fastest.
Arguments:
- adjoint: float32 [4, 125, 16384], P(None, None, ('shot', 'dom', 'sub')), parts along dimension 2, may hold values from -6 to 6
- bulk: float32 [16384], P(('shot', 'dom', 'sub')), parts along dimension 0, may hold values from 0.5 to 2
- density: float32 [16384], P(('shot', 'dom', 'sub')), parts along dimension 0, may hold values from 0.5 to 2
- neighbours: int32 [6, 16384], P(None, ('shot', 'dom', 'sub')), parts along dimension 1, may hold values from 0 to 768, as said below
- keyframe: bfloat16 [4, 125, 16384], P(None, None, ('shot', 'dom', 'sub')), parts along dimension 2, may hold values from -6 to 6
- codes: int32 [4, 125, 16384], P(None, None, ('shot', 'dom', 'sub')), parts along dimension 2, may hold values from -127 to 127
- exponents: int32 [4, 16384], P(None, ('shot', 'dom', 'sub')), parts along dimension 1, may hold values from -8 to -6
- group_elem: int32 [16384], P(('shot', 'dom', 'sub')), parts along dimension 0, may hold values from 0 to 8191, as said below
Outputs:
- update: float32 [4, 125, 16384], P(None, None, ('shot', 'dom', 'sub')), parts along dimension 2
- image: float32 [2, 125, 16384], P(None, None, ('shot', 'dom', 'sub')), parts along dimension 2
The draws below stay inside these ranges and needn't reach their ends.
There are 2 independent parts, one for each index of `shot`. The reference program is written for one: setup_inputs(seed, part) draws one part's arguments, and reference() takes and returns one part's arrays. A program takes and returns all parts, laid end to end along the dimension named above; each array names one. Nothing has to cross between parts.
Inputs may be any that keep to these rules, and one draw needn't show every extreme that they name: `neighbours`: block k holds element ids k * 512 onward; its elements are the cells of a 8 x 16 x 4 grid of unit cubes in an order of its own, cell (ix, iy, iz) with position j = ix * 16 + iy, and blocks are stacked along the third dimension in the order of k. Row f (faces -x, +x, -y, +y, -z, +z) gives the block-local index of the element across face f inside the block; for face -z of a bottom cell 512 + j, for face +z of a top cell 512 + 128 + j; 768 for faces on the block's x or y sides. Elements across a face share its nodes in the same order. `group_elem`: A permutation of all element ids. The rows of one block name at most 40 elements of any one block (ids k * 512 onward), and that many in every draw.
All inputs are finite; a program needn't handle non-finite values.
Results may differ from the reference program's by a relative error of at most 0.003.
Values may be sent and summed in bfloat16 or wider, within the bound.
A program may use at most 128 MiB of HBM per device.

```python
import math
import jax
import jax.numpy as jnp
import numpy as np
from jax import lax

GX = 8
GY = 16
GZ = 4
NODES = 125
FIELDS = 4
ORDER = 4
E_DEV = 512
BFACE = 128
NDEV = 16
ELEMS = 8192
QUOTA = 32
SPARE = 8


def draw_neighbours(key, part):
    key = jax.random.fold_in(key, 11)
    keys = jax.random.split(key, NDEV)
    labels = jax.vmap(lambda one_key: jax.random.permutation(one_key, E_DEV))(keys).astype(jnp.int32)
    cells = jnp.arange(E_DEV, dtype=jnp.int32)
    first_ix = cells // (GY * GZ)
    second_iy = cells // GZ % GY
    third_iz = cells % GZ
    position = first_ix * GY + second_iy
    outside = E_DEV + 2 * BFACE

    def per_device(label_row):

        def shifted(offset):
            return label_row[jnp.clip(cells + offset, 0, E_DEV - 1)]
        rows_out = [jnp.where(first_ix > 0, shifted(-GY * GZ), outside), jnp.where(first_ix < GX - 1, shifted(GY * GZ), outside), jnp.where(second_iy > 0, shifted(-GZ), outside), jnp.where(second_iy < GY - 1, shifted(GZ), outside), jnp.where(third_iz > 0, shifted(-1), E_DEV + position), jnp.where(third_iz < GZ - 1, shifted(1), E_DEV + BFACE + position)]
        table = jnp.stack(rows_out).astype(jnp.int32)
        return jnp.zeros((6, E_DEV), jnp.int32).at[:, label_row].set(table)
    per_block = jax.vmap(per_device)(labels)
    return jnp.transpose(per_block, (1, 0, 2)).reshape(6, NDEV * E_DEV)


def draw_group_elem(key, part):
    key = jax.random.fold_in(key, 12)
    first_key, second_key, third_key = jax.random.split(key, 3)
    order = jax.random.permutation(first_key, NDEV).astype(jnp.int32)
    block_ids = jnp.arange(NDEV, dtype=jnp.int32)
    plus_one = (block_ids[None, :] == order[:, None]).astype(jnp.int32)
    minus_one = (block_ids[None, :] == jnp.roll(order, -1)[:, None]).astype(jnp.int32)
    counts = QUOTA + SPARE * plus_one - SPARE * minus_one
    running = jnp.cumsum(counts, axis=0)
    positions = jnp.arange(E_DEV, dtype=jnp.int32)
    sources = jnp.sum((running[None, :, :] <= positions[:, None, None]).astype(jnp.int32), axis=1)
    sources = jnp.transpose(sources, (1, 0))
    dest_keys = jax.random.split(second_key, NDEV)
    inner = jax.vmap(lambda one_key: jax.random.permutation(one_key, E_DEV))(dest_keys).astype(jnp.int32)
    elements = block_ids[:, None] * E_DEV + inner
    shuffle = jax.random.permutation(third_key, ELEMS).astype(jnp.int32)
    sort_keys = sources.reshape(ELEMS) * ELEMS + shuffle
    arrangement = jnp.argsort(sort_keys, stable=True)
    return elements.reshape(ELEMS)[arrangement].astype(jnp.int32)


def with_ends(array, rng, smallest, high):
    index_at = [jax.random.randint(jax.random.fold_in(rng, axis), (), 0, length) for axis, length in enumerate(array.shape)]
    widest = array.shape.index(max(array.shape))
    neighbour = index_at[:widest] + [(index_at[widest] + 1) % array.shape[widest]] + index_at[widest + 1:]
    return array.at[tuple(index_at)].set(smallest).at[tuple(neighbour)].set(high)


def levels(own_key, extent, cuts, low, largest):
    loudness = 1.0
    for axis_at, parts in cuts:
        draws = jax.random.uniform(jax.random.fold_in(jax.random.fold_in(own_key, 6), axis_at), (parts,), jnp.float32, low / len(cuts), largest / len(cuts))
        loudness = loudness * jnp.repeat(jnp.exp(draws), extent[axis_at] // parts).reshape((-1,) + (1,) * (len(extent) - 1 - axis_at))
    return loudness


def gaussian(rng, dims, width, limit, cuts=(), kind=jnp.bfloat16):
    drawn = jax.random.normal(rng, dims, jnp.float32) * width
    if len(cuts) > 0:
        drawn = levels(rng, dims, cuts, -0.22, 0.18) * drawn
    return jnp.clip(drawn, min=-limit, max=limit).astype(kind)


def setup_inputs(seed: int = 0, part: int = 0) -> dict:
    seeds = jax.random.split(jax.random.key(seed), 9)
    part_keys = jax.random.split(jax.random.fold_in(seeds[8], part), 9)
    adjoint = gaussian(part_keys[0], (FIELDS, NODES, ELEMS), 1.0, 6.0, ((2, 16),), jnp.float32)
    bulk = jnp.clip(jnp.exp(math.log(2.0) - 1.3862944 * jax.random.uniform(part_keys[1], (ELEMS,), jnp.float32) ** levels(part_keys[1], (ELEMS,), ((0, 16),), -0.2, 0.2)), 0.5, 2.0)
    density = jnp.clip(jnp.exp(math.log(2.0) - 1.3862944 * jax.random.uniform(part_keys[2], (ELEMS,), jnp.float32) ** levels(part_keys[2], (ELEMS,), ((0, 16),), -0.2, 0.2)), 0.5, 2.0)
    neighbours = draw_neighbours(jax.random.fold_in(jax.random.fold_in(seeds[8], part), 71), part)
    keyframe = gaussian(part_keys[4], (FIELDS, NODES, ELEMS), 1.0, 6.0, ((2, 16),))
    codes = with_ends(jax.random.randint(part_keys[5], (FIELDS, NODES, ELEMS), -127, 128), jax.random.fold_in(part_keys[5], 1), -127, 127).astype(jnp.int32)
    exponents = with_ends(jax.random.randint(part_keys[6], (FIELDS, ELEMS), -8, -5), jax.random.fold_in(part_keys[6], 1), -8, (-5) - 1).astype(jnp.int32)
    group_elem = draw_group_elem(jax.random.fold_in(jax.random.fold_in(seeds[8], part), 71), part)
    return {"adjoint": adjoint, "bulk": bulk, "density": density, "neighbours": neighbours, "keyframe": keyframe, "codes": codes, "exponents": exponents, "group_elem": group_elem}


time_step = 0.04
penalty = 2.0
lift_gain = 90.0 / 7.0


def derivative_tables():
    points = np.linspace(-1.0, 1.0, 5)
    weights = np.ones(5)
    for node_idx in range(5):
        for other_idx in range(5):
            if other_idx != node_idx:
                weights[node_idx] = weights[node_idx] / (points[node_idx] - points[other_idx])
    slopes = np.zeros((5, 5))
    for row_idx in range(5):
        for col_idx in range(5):
            if row_idx != col_idx:
                slopes[row_idx, col_idx] = (weights[col_idx] / weights[row_idx]) / (points[row_idx] - points[col_idx])
        slopes[row_idx, row_idx] = -np.sum(slopes[row_idx])
    identity = np.eye(5)
    blocks = [2.0 * np.kron(np.kron(slopes, identity), identity),
              2.0 * np.kron(np.kron(identity, slopes), identity),
              2.0 * np.kron(np.kron(identity, identity), slopes)]
    return jnp.asarray(np.concatenate(blocks, 0), jnp.float32), jnp.asarray(np.concatenate(blocks, 1), jnp.float32)


def apply_operator(state, bulk, density, grad_mat, div_mat):
    elem_count = state.shape[2]
    pressure = state[0]
    velocity = state[1:].reshape(3 * NODES, elem_count)
    grad_p = jnp.dot(grad_mat, pressure, precision=lax.Precision.HIGHEST, preferred_element_type=jnp.float32).reshape(3, NODES, elem_count)
    diverge = jnp.dot(div_mat, velocity, precision=lax.Precision.HIGHEST, preferred_element_type=jnp.float32)
    new_p = -(bulk * diverge)
    new_v = -(grad_p / density)
    return jnp.concatenate([new_p[None], new_v], 0)


def predict(state, bulk, density, grad_mat, div_mat):
    series = state
    summed = state
    for power in range(1, ORDER + 1):
        series = apply_operator(series, bulk, density, grad_mat, div_mat) * (time_step / (power + 1))
        summed = summed + series
    return summed


def face_payload(state5, bulk, density, face_id):
    axis_no = face_id // 2
    node_at = 0 if face_id % 2 == 0 else 4
    signum = -1.0 if face_id % 2 == 0 else 1.0
    if axis_no == 0:
        face_trace = state5[:, node_at]
    elif axis_no == 1:
        face_trace = state5[:, :, node_at]
    else:
        face_trace = state5[:, :, :, node_at]
    face_trace = face_trace.reshape(4, 25, state5.shape[4])
    flux_p = signum * (bulk * face_trace[1 + axis_no])
    flux_v = signum * (face_trace[0] / density)
    return jnp.concatenate([face_trace, flux_p[None], flux_v[None]], 0)


def face_jump(payload, outside, axis_no):
    jump = 0.5 * penalty * (outside[:4] - payload[:4])
    jump = jump.at[0].add(0.5 * (payload[4] + outside[4]))
    jump = jump.at[1 + axis_no].add(0.5 * (payload[5] + outside[5]))
    return lift_gain * jump


def add_face(surface5, contrib, face_id):
    axis_no = face_id // 2
    node_at = 0 if face_id % 2 == 0 else 4
    block = contrib.reshape(4, 5, 5, surface5.shape[4])
    if axis_no == 0:
        return surface5.at[:, node_at].add(block)
    if axis_no == 1:
        return surface5.at[:, :, node_at].add(block)
    return surface5.at[:, :, :, node_at].add(block)


def exterior_ids(neighbours):
    local_ids = neighbours.reshape(6, NDEV, E_DEV)
    device_ids = jnp.broadcast_to(jnp.arange(NDEV, dtype=jnp.int32)[:, None], (NDEV, E_DEV))
    element_ids = jnp.broadcast_to(jnp.arange(E_DEV, dtype=jnp.int32)[None, :], (NDEV, E_DEV))

    def rim_table(slot_of):
        valid = (slot_of >= 0) & (slot_of < BFACE)
        target = jnp.where(valid, slot_of, BFACE).astype(jnp.int32)
        return jnp.zeros((NDEV, BFACE), jnp.int32).at[device_ids, target].set(element_ids, mode="drop")

    top_layer = rim_table(local_ids[5] - E_DEV - BFACE)
    bottom_layer = rim_table(local_ids[4] - E_DEV)
    rows_out = []
    for face_id in range(6):
        nearby = local_ids[face_id]
        own_ids = device_ids * E_DEV + nearby
        lower_dev = jnp.maximum(device_ids - 1, 0)
        lower_slot = jnp.clip(nearby - E_DEV, 0, BFACE - 1)
        from_lower = jnp.where(device_ids > 0, lower_dev * E_DEV + top_layer[lower_dev, lower_slot], ELEMS)
        upper_dev = jnp.minimum(device_ids + 1, NDEV - 1)
        upper_slot = jnp.clip(nearby - E_DEV - BFACE, 0, BFACE - 1)
        from_upper = jnp.where(device_ids < NDEV - 1, upper_dev * E_DEV + bottom_layer[upper_dev, upper_slot], ELEMS)
        chosen = jnp.where(nearby < E_DEV, own_ids,
                           jnp.where(nearby < E_DEV + BFACE, from_lower,
                                     jnp.where(nearby < E_DEV + 2 * BFACE, from_upper, ELEMS)))
        rows_out.append(chosen.reshape(ELEMS).astype(jnp.int32))
    return rows_out


def reference(adjoint, bulk, density, neighbours, keyframe, codes, exponents, group_elem):
    grad_mat, div_mat = derivative_tables()
    scale_factor = jnp.exp2(exponents.astype(jnp.float32))
    decoded = (keyframe.astype(jnp.float32) + codes.astype(jnp.float32) * scale_factor[:, None, :]).astype(jnp.bfloat16)
    snapshot = jnp.zeros((FIELDS, NODES, ELEMS), jnp.bfloat16).at[:, :, group_elem.astype(jnp.int32)].set(decoded)
    summed = predict(adjoint, bulk, density, grad_mat, div_mat)
    state5 = summed.reshape(FIELDS, 5, 5, 5, ELEMS)
    payloads = [face_payload(state5, bulk, density, face_id) for face_id in range(6)]
    global_ids = exterior_ids(neighbours)
    zero_column = jnp.zeros((6, 25, 1), jnp.float32)
    surface5 = jnp.zeros((FIELDS, 5, 5, 5, ELEMS), jnp.float32)
    for face_id in range(6):
        table = jnp.concatenate([payloads[face_id ^ 1], zero_column], 2)
        outside = jnp.take(table, global_ids[face_id], axis=2)
        surface5 = add_face(surface5, face_jump(payloads[face_id], outside, face_id // 2), face_id)
    update = time_step * (apply_operator(summed, bulk, density, grad_mat, div_mat) + surface5.reshape(FIELDS, NODES, ELEMS))
    snap_full = snapshot.astype(jnp.float32)
    image_bulk = snap_full[0] * summed[0]
    image_density = snap_full[1] * summed[1] + snap_full[2] * summed[2] + snap_full[3] * summed[3]
    return update, jnp.stack([image_bulk, image_density], 0)
```

```python
import functools

import jax
import jax.numpy as jnp
import numpy as np
from jax import lax
from jax.experimental import pallas as pl
from jax.experimental.pallas import tpu as pltpu
from jax.sharding import PartitionSpec as P

GX = 8
GY = 16
NODES = 125
FIELDS = 4
ORDER = 4
ROWS = 128
FROWS = 32

time_step = 0.04
lift_gain = 90.0 / 7.0

F32 = jnp.float32
BF16 = jnp.bfloat16
MESH = pl.DeviceIdType.MESH


def tables():
    points = np.linspace(-1.0, 1.0, 5)
    weights = np.ones(5)
    for i in range(5):
        for j in range(5):
            if i != j:
                weights[i] = weights[i] / (points[i] - points[j])
    slopes = np.zeros((5, 5))
    for i in range(5):
        for j in range(5):
            if i != j:
                slopes[i, j] = weights[j] / weights[i] / (points[i] - points[j])
        slopes[i, i] = -np.sum(slopes[i])
    whole = np.round(6.0 * slopes)
    eye = np.eye(5)
    ops = [
        np.kron(np.kron(whole, eye), eye),
        np.kron(np.kron(eye, whole), eye),
        np.kron(np.kron(eye, eye), whole),
    ]
    padded = [np.pad(op, ((0, 3), (0, 3))) for op in ops]
    grad = np.concatenate(padded, 0)
    grad = np.concatenate([grad, grad], 1)
    div = np.concatenate([padded[i // 2] for i in range(6)], 1)
    select = np.zeros((6 * FROWS, ROWS))
    grid = np.arange(NODES).reshape(5, 5, 5)
    for face in range(6):
        at = 0 if face % 2 == 0 else 4
        nodes = np.take(grid, at, axis=face // 2).reshape(25)
        select[face * FROWS + np.arange(25), nodes] = 1.0
    pick = np.concatenate([select, select], 1)
    place = np.concatenate([select.T, select.T], 1)
    place_rim = select.T[:, 4 * FROWS :]
    return tuple(jnp.asarray(m, BF16) for m in (grad, div, pick, place, place_rim))


def dot(a, b):
    return lax.dot_general(a, b, (((1,), (0,)), ((), ())), preferred_element_type=F32)


def split(value):
    high = value.astype(BF16)
    return high, (value - high.astype(F32)).astype(BF16)


def kernel(
    devices,
    subs,
    cap,
    adj_ref,
    bulk_ref,
    rho_ref,
    nb_ref,
    key_ref,
    code_ref,
    exp_ref,
    grp_ref,
    grad_ref,
    div_ref,
    pick_ref,
    place_ref,
    place_rim_ref,
    upd_ref,
    img_ref,
    dec_ref,
    hl_ref,
    acc_ref,
    w_ref,
    u_ref,
    j_ref,
    send_ref,
    recv_ref,
    rim_out,
    rim_in,
    send_sem,
    recv_sem,
    rim_send_sem,
    rim_recv_sem,
):
    elems = adj_ref.shape[2]
    rim = GX * GY
    me = lax.axis_index("dom") * subs + lax.axis_index("sub")

    def place_of(index):
        return {"dom": index // subs, "sub": index % subs}

    barrier = pltpu.get_barrier_semaphore()

    def greet(k, carry):
        other = lax.rem(me + k, devices)
        pl.semaphore_signal(barrier, inc=1, device_id=place_of(other), device_id_type=MESH)
        return carry

    lax.fori_loop(1, devices, greet, 0)

    group = grp_ref[...]
    owner = lax.div(group, jnp.int32(elems))
    ident = lax.rem(group, jnp.int32(elems)) + 1
    scale = jnp.exp2(exp_ref[...].astype(F32))
    for f in range(FIELDS):
        dec_ref[f, 0:NODES, :] = (
            key_ref[f].astype(F32) + code_ref[f].astype(F32) * scale[f : f + 1]
        )
        dec_ref[f, NODES:ROWS, :] = jnp.zeros((ROWS - NODES, elems), F32)
    dec_ref[0, NODES : NODES + 1, :] = lax.shift_right_logical(ident, 4).astype(F32)
    dec_ref[0, NODES + 1 : NODES + 2, :] = (ident & 15).astype(F32)
    decoded = dec_ref[...].astype(BF16).reshape(FIELDS * ROWS, elems)

    owned = lax.broadcasted_iota(jnp.int32, (devices, elems), 0) == owner
    owned_f = owned.astype(F32)
    before = (
        lax.broadcasted_iota(jnp.int32, (elems, elems), 0)
        < lax.broadcasted_iota(jnp.int32, (elems, elems), 1)
    )
    earlier = dot(owned_f.astype(BF16), before.astype(F32).astype(BF16))
    rank = jnp.sum(earlier * owned_f, axis=0, keepdims=True).astype(jnp.int32)
    slot = owner * cap + rank
    chosen = (lax.broadcasted_iota(jnp.int32, (devices * cap, elems), 0) == slot).astype(F32)
    outgoing = lax.dot_general(
        chosen.astype(BF16), decoded, (((1,), (1,)), ((), ())), preferred_element_type=F32
    )
    outgoing = jnp.concatenate(
        [outgoing[:, f * ROWS : (f + 1) * ROWS].reshape(devices, cap, ROWS) for f in range(FIELDS)],
        axis=1,
    )
    send_ref[...] = outgoing.astype(BF16)
    recv_ref[me] = send_ref[me]

    pl.semaphore_wait(barrier, devices - 1)

    def row_copy(k, landing):
        other = lax.rem(me + k, devices)
        return pltpu.make_async_remote_copy(
            src_ref=send_ref.at[other],
            dst_ref=recv_ref.at[landing(other)],
            send_sem=send_sem.at[k],
            recv_sem=recv_sem.at[landing(other)],
            device_id=place_of(other),
            device_id_type=MESH,
        )

    def start_rows(k, carry):
        row_copy(k, lambda other: me).start()
        return carry

    lax.fori_loop(1, devices, start_rows, 0)

    bulk = bulk_ref[...]
    inverse = 1.0 / rho_ref[...]

    def store_split(f, value):
        high, low = split(value)
        hl_ref[2 * f * ROWS : (2 * f + 1) * ROWS, :] = high
        hl_ref[(2 * f + 1) * ROWS : (2 * f + 2) * ROWS, :] = low

    def operator(gain):
        grad = dot(grad_ref[...], hl_ref[0 : 2 * ROWS, :])
        diverge = dot(div_ref[...], hl_ref[2 * ROWS :, :])
        by_bulk = bulk * (-gain / 3.0)
        by_rho = inverse * (-gain / 3.0)
        return [by_bulk * diverge] + [
            by_rho * grad[i * ROWS : (i + 1) * ROWS] for i in range(3)
        ]

    for f in range(FIELDS):
        acc_ref[f, 0:NODES, :] = adj_ref[f]
        acc_ref[f, NODES:ROWS, :] = jnp.zeros((ROWS - NODES, elems), F32)
    for f in range(FIELDS):
        store_split(f, acc_ref[f])
    for power in range(1, ORDER + 1):
        series = operator(time_step / (power + 1))
        for f in range(FIELDS):
            total = acc_ref[f] + series[f]
            acc_ref[f] = total
            store_split(f, total if power == ORDER else series[f])

    traces = [dot(pick_ref[...], hl_ref[2 * f * ROWS : (2 * f + 2) * ROWS, :]) for f in range(FIELDS)]
    half_bulk = 0.5 * bulk
    half_inverse = 0.5 * inverse
    for face in range(6):
        axis = face // 2
        sign = -1.0 if face % 2 == 0 else 1.0
        rows = [t[face * FROWS : (face + 1) * FROWS] for t in traces]
        flux_p = (sign * half_bulk) * rows[1 + axis]
        flux_v = (sign * half_inverse) * rows[0]
        for f in range(FIELDS):
            flux = flux_p if f == 0 else flux_v if f == 1 + axis else None
            given = rows[f] if flux is None else rows[f] + flux
            kept = rows[f] if flux is None else rows[f] - flux
            high, low = split(given)
            w_ref[face, f * FROWS : (f + 1) * FROWS, :] = high
            w_ref[face, ROWS + f * FROWS : ROWS + (f + 1) * FROWS, :] = low
            u_ref[face, f * FROWS : (f + 1) * FROWS, :] = kept

    rim_cell = lax.broadcasted_iota(jnp.int32, (rim, elems), 0)
    rim_hot = [
        (rim_cell + (elems + side * rim) == nb_ref[4 + side : 5 + side, :]).astype(F32).astype(BF16)
        for side in range(2)
    ]
    for side in range(2):
        rim_out[side] = lax.dot_general(
            w_ref[4 + side, 0:ROWS, :],
            rim_hot[side],
            (((1,), (1,)), ((), ())),
            preferred_element_type=F32,
        ).astype(BF16)

    def rim_copy(side, other):
        return pltpu.make_async_remote_copy(
            src_ref=rim_out.at[side],
            dst_ref=rim_in.at[1 - side],
            send_sem=rim_send_sem.at[side],
            recv_sem=rim_recv_sem.at[1 - side],
            device_id=place_of(other),
            device_id_type=MESH,
        )

    has_below = me > 0
    has_above = me < devices - 1

    @pl.when(has_below)
    def _():
        rim_copy(0, me - 1).start()

    @pl.when(has_above)
    def _():
        rim_copy(1, me + 1).start()

    @pl.when(me == 0)
    def _():
        rim_in[0] = jnp.zeros((ROWS, rim), BF16)

    @pl.when(me == devices - 1)
    def _():
        rim_in[1] = jnp.zeros((ROWS, rim), BF16)

    volume = operator(time_step)
    for f in range(FIELDS):
        upd_ref[f] = volume[f][0:NODES]

    cell = lax.broadcasted_iota(jnp.int32, (elems, elems), 0)
    for face in range(6):
        hot = (cell == nb_ref[face : face + 1, :]).astype(F32).astype(BF16)
        both = dot(w_ref[face ^ 1], hot)
        jump = both[0:ROWS] + both[ROWS:] - u_ref[face]
        for f in range(FIELDS):
            high, low = split(jump[f * FROWS : (f + 1) * FROWS])
            j_ref[f, face * FROWS : (face + 1) * FROWS, :] = high
            j_ref[f, (6 + face) * FROWS : (7 + face) * FROWS, :] = low
    for f in range(FIELDS):
        surface = dot(place_ref[...], j_ref[f])
        upd_ref[f] = upd_ref[f] + (time_step * lift_gain) * surface[0:NODES]

    @pl.when(has_above)
    def _():
        rim_copy(0, me + 1).wait_recv()

    @pl.when(has_below)
    def _():
        rim_copy(1, me - 1).wait_recv()

    outer = [dot(rim_in[side], rim_hot[side]).astype(BF16) for side in range(2)]
    for f in range(FIELDS):
        part = jnp.concatenate([o[f * FROWS : (f + 1) * FROWS] for o in outer], axis=0)
        surface = dot(place_rim_ref[...], part)
        upd_ref[f] = upd_ref[f] + (time_step * lift_gain) * surface[0:NODES]

    def wait_rows(k, carry):
        row_copy(k, lambda other: other).wait_recv()
        return carry

    lax.fori_loop(1, devices, wait_rows, 0)
    arrived = recv_ref[...].astype(F32)
    arrived = jnp.concatenate(
        [
            arrived[:, f * cap : (f + 1) * cap, :].reshape(devices * cap, ROWS)
            for f in range(FIELDS)
        ],
        axis=1,
    )
    target = arrived[:, NODES : NODES + 1] * 16.0 + arrived[:, NODES + 1 : NODES + 2] - 1.0
    hot = (
        lax.broadcasted_iota(jnp.int32, (devices * cap, elems), 1) == target.astype(jnp.int32)
    ).astype(F32)
    snapshot = lax.dot_general(
        arrived.astype(BF16),
        hot.astype(BF16),
        (((0,), (0,)), ((), ())),
        preferred_element_type=F32,
    )
    product = [snapshot[f * ROWS : (f + 1) * ROWS] * acc_ref[f] for f in range(FIELDS)]
    img_ref[0] = product[0][0:NODES]
    img_ref[1] = (product[1] + product[2] + product[3])[0:NODES]

    def wait_sent(k, carry):
        row_copy(k, lambda other: me).wait_send()
        return carry

    lax.fori_loop(1, devices, wait_sent, 0)

    @pl.when(has_below)
    def _():
        rim_copy(0, me - 1).wait_send()

    @pl.when(has_above)
    def _():
        rim_copy(1, me + 1).wait_send()


def local(adjoint, bulk, density, neighbours, keyframe, codes, exponents, group_elem):
    elems = adjoint.shape[2]
    devices = lax.axis_size(("dom", "sub"))
    subs = lax.axis_size("sub")
    rim = GX * GY
    mean = elems // devices
    cap = -(-(mean + mean // 4) // 8) * 8
    packed = FIELDS * cap
    vmem = pl.BlockSpec(memory_space=pltpu.VMEM)
    return pl.pallas_call(
        functools.partial(kernel, devices, subs, cap),
        out_shape=(
            jax.ShapeDtypeStruct((FIELDS, NODES, elems), F32),
            jax.ShapeDtypeStruct((2, NODES, elems), F32),
        ),
        in_specs=[vmem] * 13,
        out_specs=(vmem, vmem),
        scratch_shapes=[
            pltpu.VMEM((FIELDS, ROWS, elems), F32),
            pltpu.VMEM((2 * FIELDS * ROWS, elems), BF16),
            pltpu.VMEM((FIELDS, ROWS, elems), F32),
            pltpu.VMEM((6, 2 * ROWS, elems), BF16),
            pltpu.VMEM((6, ROWS, elems), F32),
            pltpu.VMEM((FIELDS, 12 * FROWS, elems), BF16),
            pltpu.VMEM((devices, packed, ROWS), BF16),
            pltpu.VMEM((devices, packed, ROWS), BF16),
            pltpu.VMEM((2, ROWS, rim), BF16),
            pltpu.VMEM((2, ROWS, rim), BF16),
            pltpu.SemaphoreType.DMA((devices,)),
            pltpu.SemaphoreType.DMA((devices,)),
            pltpu.SemaphoreType.DMA((2,)),
            pltpu.SemaphoreType.DMA((2,)),
        ],
        compiler_params=pltpu.CompilerParams(
            collective_id=0, has_side_effects=True, vmem_limit_bytes=48 * 1024 * 1024
        ),
    )(
        adjoint,
        bulk.reshape(1, elems),
        density.reshape(1, elems),
        neighbours,
        keyframe,
        codes,
        exponents,
        group_elem.reshape(1, elems),
        *tables(),
    )


def solution(mesh):
    placed = (
        P(None, None, ("shot", "dom", "sub")),
        P(("shot", "dom", "sub")),
        P(("shot", "dom", "sub")),
        P(None, ("shot", "dom", "sub")),
        P(None, None, ("shot", "dom", "sub")),
        P(None, None, ("shot", "dom", "sub")),
        P(None, ("shot", "dom", "sub")),
        P(("shot", "dom", "sub")),
    )
    return jax.shard_map(
        local,
        mesh=mesh,
        in_specs=placed,
        out_specs=(P(None, None, ("shot", "dom", "sub")), P(None, None, ("shot", "dom", "sub"))),
        check_vma=False,
    )
```

```python
import functools

import jax
import jax.numpy as jnp
import numpy as np
from jax import lax
from jax.experimental import pallas as pl
from jax.experimental.pallas import tpu as pltpu
from jax.sharding import PartitionSpec as P

GX = 8
GY = 16
NODES = 125
FIELDS = 4
ORDER = 4
ROWS = 128
FROWS = 32

time_step = 0.04
lift_gain = 90.0 / 7.0

F32 = jnp.float32
BF16 = jnp.bfloat16
MESH = pl.DeviceIdType.MESH


def tables():
    points = np.linspace(-1.0, 1.0, 5)
    weights = np.ones(5)
    for i in range(5):
        for j in range(5):
            if i != j:
                weights[i] = weights[i] / (points[i] - points[j])
    slopes = np.zeros((5, 5))
    for i in range(5):
        for j in range(5):
            if i != j:
                slopes[i, j] = weights[j] / weights[i] / (points[i] - points[j])
        slopes[i, i] = -np.sum(slopes[i])
    whole = np.round(6.0 * slopes)
    eye = np.eye(5)
    ops = [
        np.kron(np.kron(whole, eye), eye),
        np.kron(np.kron(eye, whole), eye),
        np.kron(np.kron(eye, eye), whole),
    ]
    padded = [np.pad(op, ((0, 3), (0, 3))) for op in ops]
    grad = np.concatenate(padded, 0)
    grad = np.concatenate([grad, grad], 1)
    select = np.zeros((6 * FROWS, ROWS))
    grid = np.arange(NODES).reshape(5, 5, 5)
    for face in range(6):
        at = 0 if face % 2 == 0 else 4
        nodes = np.take(grid, at, axis=face // 2).reshape(25)
        select[face * FROWS + np.arange(25), nodes] = 1.0
    pick = np.concatenate([select, select], 1)
    place = np.concatenate([select.T, select.T[:, 4 * FROWS :]], 1)
    return jnp.asarray(np.concatenate([grad, pick, place], 0), BF16)


def dot(a, b):
    return lax.dot_general(a, b, (((1,), (0,)), ((), ())), preferred_element_type=F32)


def split(value):
    high = value.astype(BF16)
    return high, (value - high.astype(F32)).astype(BF16)


def kernel(
    devices,
    subs,
    cap,
    bulk_ref,
    rho_ref,
    nb_ref,
    grp_ref,
    coded_ref,
    adj_ref,
    table_ref,
    upd_ref,
    img_ref,
    dec_ref,
    hl_ref,
    acc_ref,
    sum_ref,
    w_ref,
    u_ref,
    j_ref,
    send_ref,
    recv_ref,
    rim_out,
    rim_in,
    send_sem,
    recv_sem,
    rim_send_sem,
    rim_recv_sem,
):
    elems = adj_ref.shape[2]
    rim = GX * GY
    half = devices // 2
    me = lax.axis_index("dom") * subs + lax.axis_index("sub")
    my_base = (me // half) * half
    far_base = half - my_base

    def place_of(index):
        return {"dom": index // subs, "sub": index % subs}

    barrier = pltpu.get_barrier_semaphore()

    def greet(k, carry):
        other = lax.rem(me + k, devices)
        pl.semaphore_signal(barrier, inc=1, device_id=place_of(other), device_id_type=MESH)
        return carry

    lax.fori_loop(1, devices, greet, 0)

    group = grp_ref[...]
    owner = lax.div(group, jnp.int32(elems))
    ident = lax.rem(group, jnp.int32(elems)) + 1
    owned = lax.broadcasted_iota(jnp.int32, (devices, elems), 0) == owner
    owned_f = owned.astype(F32)
    before = (
        lax.broadcasted_iota(jnp.int32, (elems, elems), 0)
        < lax.broadcasted_iota(jnp.int32, (elems, elems), 1)
    )
    earlier = dot(owned_f.astype(BF16), before.astype(F32).astype(BF16))
    rank = jnp.sum(earlier * owned_f, axis=0, keepdims=True).astype(jnp.int32)
    slot = owner * cap + rank

    dec_ref[:, 0:NODES, :] = jnp.swapaxes(coded_ref[...].astype(F32), 0, 1)
    for f in range(FIELDS):
        dec_ref[f, NODES:ROWS, :] = jnp.zeros((ROWS - NODES, elems), F32)
    dec_ref[0, NODES : NODES + 1, :] = lax.shift_right_logical(ident, 4).astype(F32)
    dec_ref[0, NODES + 1 : NODES + 2, :] = (ident & 15).astype(F32)
    decoded = dec_ref[...].astype(BF16).reshape(FIELDS * ROWS, elems)

    def dispatch(base):
        cell = lax.broadcasted_iota(jnp.int32, (half * cap, elems), 0) + base * cap
        rows = lax.dot_general(
            (cell == slot).astype(F32).astype(BF16),
            decoded,
            (((1,), (1,)), ((), ())),
            preferred_element_type=F32,
        )
        rows = jnp.concatenate(
            [rows[:, f * ROWS : (f + 1) * ROWS].reshape(half, cap, ROWS) for f in range(FIELDS)],
            axis=1,
        )
        send_ref[pl.ds(base, half)] = rows.astype(BF16)

    def far(k):
        return far_base + lax.rem(me + k, half)

    def near(k):
        return my_base + lax.rem(me + k, half)

    def row_copy(other, landing):
        return pltpu.make_async_remote_copy(
            src_ref=send_ref.at[other],
            dst_ref=recv_ref.at[landing],
            send_sem=send_sem.at[other],
            recv_sem=recv_sem.at[landing],
            device_id=place_of(other),
            device_id_type=MESH,
        )

    def start_rows(k, carry):
        row_copy(lax.rem(me + k, devices), me).start()
        return carry

    dispatch(far_base)
    dispatch(my_base)
    pl.semaphore_wait(barrier, devices - 1)
    ahead = (5 * devices) // 8
    lax.fori_loop(1, ahead, start_rows, 0)
    recv_ref[me] = send_ref[me]

    bulk = bulk_ref[...]
    inverse = 1.0 / rho_ref[...]

    def store_split(f, value):
        high, low = split(value)
        hl_ref[2 * f * ROWS : (2 * f + 1) * ROWS, :] = high
        hl_ref[(2 * f + 1) * ROWS : (2 * f + 2) * ROWS, :] = low

    def operator(gain):
        grad = dot(table_ref[0 : 3 * ROWS, :], hl_ref[0 : 2 * ROWS, :])
        diverge = sum(
            dot(
                table_ref[i * ROWS : (i + 1) * ROWS, :],
                hl_ref[2 * (i + 1) * ROWS : 2 * (i + 2) * ROWS, :],
            )
            for i in range(3)
        )
        by_bulk = bulk * (-gain / 3.0)
        by_rho = inverse * (-gain / 3.0)
        return [by_bulk * diverge] + [
            by_rho * grad[i * ROWS : (i + 1) * ROWS] for i in range(3)
        ]

    acc_ref[:, 0:NODES, :] = jnp.swapaxes(adj_ref[...], 0, 1)
    for f in range(FIELDS):
        acc_ref[f, NODES:ROWS, :] = jnp.zeros((ROWS - NODES, elems), F32)
    for f in range(FIELDS):
        store_split(f, acc_ref[f])
    for power in range(1, ORDER + 1):
        series = operator(time_step / (power + 1))
        for f in range(FIELDS):
            total = acc_ref[f] + series[f]
            acc_ref[f] = total
            store_split(f, total if power == ORDER else series[f])

    pick = table_ref[3 * ROWS : 3 * ROWS + 6 * FROWS, :]
    place = table_ref[3 * ROWS + 6 * FROWS :, :]
    traces = [dot(pick, hl_ref[2 * f * ROWS : (2 * f + 2) * ROWS, :]) for f in range(FIELDS)]
    half_bulk = 0.5 * bulk
    half_inverse = 0.5 * inverse
    for face in range(6):
        axis = face // 2
        sign = -1.0 if face % 2 == 0 else 1.0
        rows = [t[face * FROWS : (face + 1) * FROWS] for t in traces]
        flux_p = (sign * half_bulk) * rows[1 + axis]
        flux_v = (sign * half_inverse) * rows[0]
        for f in range(FIELDS):
            flux = flux_p if f == 0 else flux_v if f == 1 + axis else None
            given = rows[f] if flux is None else rows[f] + flux
            kept = rows[f] if flux is None else rows[f] - flux
            high, low = split(given)
            w_ref[face, f * FROWS : (f + 1) * FROWS, :] = high
            w_ref[face, ROWS + f * FROWS : ROWS + (f + 1) * FROWS, :] = low
            u_ref[face, f * FROWS : (f + 1) * FROWS, :] = kept

    rim_cell = lax.broadcasted_iota(jnp.int32, (rim, elems), 0)
    rim_hot = [
        (rim_cell + (elems + side * rim) == nb_ref[4 + side : 5 + side, :]).astype(F32).astype(BF16)
        for side in range(2)
    ]
    for side in range(2):
        rim_out[side] = lax.dot_general(
            w_ref[4 + side, 0:ROWS, :],
            rim_hot[side],
            (((1,), (1,)), ((), ())),
            preferred_element_type=F32,
        ).astype(BF16)

    def rim_copy(side, other):
        return pltpu.make_async_remote_copy(
            src_ref=rim_out.at[side],
            dst_ref=rim_in.at[1 - side],
            send_sem=rim_send_sem.at[side],
            recv_sem=rim_recv_sem.at[1 - side],
            device_id=place_of(other),
            device_id_type=MESH,
        )

    has_below = me > 0
    has_above = me < devices - 1

    @pl.when(has_below)
    def _():
        rim_copy(0, me - 1).start()

    @pl.when(has_above)
    def _():
        rim_copy(1, me + 1).start()

    lax.fori_loop(ahead, devices, start_rows, 0)

    @pl.when(me == 0)
    def _():
        rim_in[0] = jnp.zeros((ROWS, rim), BF16)

    @pl.when(me == devices - 1)
    def _():
        rim_in[1] = jnp.zeros((ROWS, rim), BF16)

    volume = operator(time_step)
    for f in range(FIELDS):
        sum_ref[f] = volume[f]

    cell = lax.broadcasted_iota(jnp.int32, (elems, elems), 0)
    for face in range(6):
        hot = (cell == nb_ref[face : face + 1, :]).astype(F32).astype(BF16)
        both = dot(w_ref[face ^ 1], hot)
        jump = both[0:ROWS] + both[ROWS:] - u_ref[face]
        for f in range(FIELDS):
            high, low = split(jump[f * FROWS : (f + 1) * FROWS])
            j_ref[f, face * FROWS : (face + 1) * FROWS, :] = high
            j_ref[f, (8 + face) * FROWS : (9 + face) * FROWS, :] = low
    for f in range(FIELDS):
        sum_ref[f] = sum_ref[f] + (time_step * lift_gain) * dot(
            place[:, 0 : 6 * FROWS], j_ref[f, 8 * FROWS : 14 * FROWS, :]
        )

    @pl.when(has_above)
    def _():
        rim_copy(0, me + 1).wait_recv()

    @pl.when(has_below)
    def _():
        rim_copy(1, me - 1).wait_recv()

    outer = [dot(rim_in[side], rim_hot[side]).astype(BF16) for side in range(2)]
    for f in range(FIELDS):
        for side in range(2):
            j_ref[f, (6 + side) * FROWS : (7 + side) * FROWS, :] = outer[side][
                f * FROWS : (f + 1) * FROWS
            ]
        sum_ref[f] = sum_ref[f] + (time_step * lift_gain) * dot(
            place, j_ref[f, 0 : 8 * FROWS, :]
        )
    upd_ref[...] = jnp.swapaxes(sum_ref[:, 0:NODES, :], 0, 1)

    def scatter(base):
        arrived = recv_ref[pl.ds(base, half)].astype(F32)
        arrived = jnp.concatenate(
            [
                arrived[:, f * cap : (f + 1) * cap, :].reshape(half * cap, ROWS)
                for f in range(FIELDS)
            ],
            axis=1,
        )
        target = arrived[:, NODES : NODES + 1] * 16.0 + arrived[:, NODES + 1 : NODES + 2] - 1.0
        hot = (
            lax.broadcasted_iota(jnp.int32, (half * cap, elems), 1) == target.astype(jnp.int32)
        ).astype(F32)
        return lax.dot_general(
            arrived.astype(BF16),
            hot.astype(BF16),
            (((0,), (0,)), ((), ())),
            preferred_element_type=F32,
        )

    def wait_near(k, carry):
        other = near(k)
        row_copy(other, other).wait_recv()
        return carry

    def wait_far(k, carry):
        other = far(k)
        row_copy(other, other).wait_recv()
        return carry

    lax.fori_loop(1, half, wait_near, 0)
    dec_ref[...] = scatter(my_base).reshape(FIELDS, ROWS, elems)
    lax.fori_loop(0, half, wait_far, 0)
    snapshot = scatter(far_base)
    product = [
        (snapshot[f * ROWS : (f + 1) * ROWS] + dec_ref[f]) * acc_ref[f] for f in range(FIELDS)
    ]
    image = jnp.stack([product[0], product[1] + product[2] + product[3]], axis=0)
    img_ref[...] = jnp.swapaxes(image[:, 0:NODES, :], 0, 1)

    def wait_sent(k, carry):
        other = lax.rem(me + k, devices)
        row_copy(other, me).wait_send()
        return carry

    lax.fori_loop(1, devices, wait_sent, 0)

    @pl.when(has_below)
    def _():
        rim_copy(0, me - 1).wait_send()

    @pl.when(has_above)
    def _():
        rim_copy(1, me + 1).wait_send()


def local(adjoint, bulk, density, neighbours, keyframe, codes, exponents, group_elem):
    elems = adjoint.shape[2]
    devices = lax.axis_size(("dom", "sub"))
    subs = lax.axis_size("sub")
    rim = GX * GY
    mean = elems // devices
    cap = -(-(mean + mean // 4) // 8) * 8
    packed = FIELDS * cap
    vmem = pl.BlockSpec(memory_space=pltpu.VMEM)
    shift = jnp.maximum(exponents[:, None, :], codes - 256) + 8
    delta = lax.shift_left(codes, shift)
    coded = (keyframe.astype(F32) + delta.astype(F32) * 2.0**-8).astype(BF16)
    update, image = pl.pallas_call(
        functools.partial(kernel, devices, subs, cap),
        out_shape=(
            jax.ShapeDtypeStruct((NODES, FIELDS, elems), F32),
            jax.ShapeDtypeStruct((NODES, 2, elems), F32),
        ),
        in_specs=[vmem] * 7,
        out_specs=(vmem, vmem),
        scratch_shapes=[
            pltpu.VMEM((FIELDS, ROWS, elems), F32),
            pltpu.VMEM((2 * FIELDS * ROWS, elems), BF16),
            pltpu.VMEM((FIELDS, ROWS, elems), F32),
            pltpu.VMEM((FIELDS, ROWS, elems), F32),
            pltpu.VMEM((6, 2 * ROWS, elems), BF16),
            pltpu.VMEM((6, ROWS, elems), F32),
            pltpu.VMEM((FIELDS, 14 * FROWS, elems), BF16),
            pltpu.VMEM((devices, packed, ROWS), BF16),
            pltpu.VMEM((devices, packed, ROWS), BF16),
            pltpu.VMEM((2, ROWS, rim), BF16),
            pltpu.VMEM((2, ROWS, rim), BF16),
            pltpu.SemaphoreType.DMA((devices,)),
            pltpu.SemaphoreType.DMA((devices,)),
            pltpu.SemaphoreType.DMA((2,)),
            pltpu.SemaphoreType.DMA((2,)),
        ],
        compiler_params=pltpu.CompilerParams(
            collective_id=0, has_side_effects=True, vmem_limit_bytes=40 * 1024 * 1024
        ),
    )(
        bulk.reshape(1, elems),
        density.reshape(1, elems),
        neighbours,
        group_elem.reshape(1, elems),
        jnp.swapaxes(coded, 0, 1),
        jnp.swapaxes(adjoint, 0, 1),
        tables(),
    )
    return jnp.swapaxes(update, 0, 1), jnp.swapaxes(image, 0, 1)


def solution(mesh):
    placed = (
        P(None, None, ("shot", "dom", "sub")),
        P(("shot", "dom", "sub")),
        P(("shot", "dom", "sub")),
        P(None, ("shot", "dom", "sub")),
        P(None, None, ("shot", "dom", "sub")),
        P(None, None, ("shot", "dom", "sub")),
        P(None, ("shot", "dom", "sub")),
        P(("shot", "dom", "sub")),
    )
    return jax.shard_map(
        local,
        mesh=mesh,
        in_specs=placed,
        out_specs=(P(None, None, ("shot", "dom", "sub")), P(None, None, ("shot", "dom", "sub"))),
        check_vma=False,
    )
```

```python
import functools

import jax
import jax.numpy as jnp
import numpy as np
from jax import lax
from jax.experimental import pallas as pl
from jax.experimental.pallas import tpu as pltpu
from jax.sharding import PartitionSpec as P

GX = 8
GY = 16
NODES = 125
FIELDS = 4
ORDER = 4
ROWS = 128
FROWS = 32

time_step = 0.04
lift_gain = 90.0 / 7.0

F32 = jnp.float32
BF16 = jnp.bfloat16
MESH = pl.DeviceIdType.MESH


def tables():
    points = np.linspace(-1.0, 1.0, 5)
    weights = np.ones(5)
    for i in range(5):
        for j in range(5):
            if i != j:
                weights[i] = weights[i] / (points[i] - points[j])
    slopes = np.zeros((5, 5))
    for i in range(5):
        for j in range(5):
            if i != j:
                slopes[i, j] = weights[j] / weights[i] / (points[i] - points[j])
        slopes[i, i] = -np.sum(slopes[i])
    whole = np.round(6.0 * slopes)
    eye = np.eye(5)
    ops = [
        np.kron(np.kron(whole, eye), eye),
        np.kron(np.kron(eye, whole), eye),
        np.kron(np.kron(eye, eye), whole),
    ]
    padded = [np.pad(op, ((0, 3), (0, 3))) for op in ops]
    grad = np.concatenate(padded, 0)
    grad = np.concatenate([grad, grad], 1)
    select = np.zeros((6 * FROWS, ROWS))
    grid = np.arange(NODES).reshape(5, 5, 5)
    for face in range(6):
        at = 0 if face % 2 == 0 else 4
        nodes = np.take(grid, at, axis=face // 2).reshape(25)
        select[face * FROWS + np.arange(25), nodes] = 1.0
    pick = np.concatenate([select, select], 1)
    place = np.concatenate([select.T, select.T[:, 4 * FROWS :]], 1)
    return jnp.asarray(np.concatenate([grad, pick, place], 0), BF16)


def dot(a, b):
    return lax.dot_general(a, b, (((1,), (0,)), ((), ())), preferred_element_type=F32)


def split(value):
    high = value.astype(BF16)
    return high, (value - high.astype(F32)).astype(BF16)


def kernel(
    devices,
    subs,
    cap,
    bulk_ref,
    rho_ref,
    nb_ref,
    grp_ref,
    coded_ref,
    adj_ref,
    table_ref,
    upd_ref,
    img_ref,
    dec_ref,
    hl_ref,
    acc_ref,
    sum_ref,
    w_ref,
    u_ref,
    j_ref,
    send_ref,
    recv_ref,
    rim_out,
    rim_in,
    send_sem,
    recv_sem,
    rim_send_sem,
    rim_recv_sem,
):
    elems = adj_ref.shape[2]
    rim = GX * GY
    half = devices // 2
    me = lax.axis_index("dom") * subs + lax.axis_index("sub")
    my_base = (me // half) * half
    far_base = half - my_base

    def place_of(index):
        return {"dom": index // subs, "sub": index % subs}

    barrier = pltpu.get_barrier_semaphore()

    def greet(k, carry):
        other = lax.rem(me + k, devices)
        pl.semaphore_signal(barrier, inc=1, device_id=place_of(other), device_id_type=MESH)
        return carry

    lax.fori_loop(1, devices, greet, 0)

    group = grp_ref[...]
    owner = lax.div(group, jnp.int32(elems))
    ident = lax.rem(group, jnp.int32(elems)) + 1
    owned = lax.broadcasted_iota(jnp.int32, (devices, elems), 0) == owner
    owned_f = owned.astype(F32)
    before = (
        lax.broadcasted_iota(jnp.int32, (elems, elems), 0)
        < lax.broadcasted_iota(jnp.int32, (elems, elems), 1)
    )
    earlier = dot(owned_f.astype(BF16), before.astype(F32).astype(BF16))
    rank = jnp.sum(earlier * owned_f, axis=0, keepdims=True).astype(jnp.int32)
    slot = owner * cap + rank

    dec_ref[:, 0:NODES, :] = jnp.swapaxes(coded_ref[...].astype(F32), 0, 1)
    for f in range(FIELDS):
        dec_ref[f, NODES:ROWS, :] = jnp.zeros((ROWS - NODES, elems), F32)
    dec_ref[0, NODES : NODES + 1, :] = lax.shift_right_logical(ident, 4).astype(F32)
    dec_ref[0, NODES + 1 : NODES + 2, :] = (ident & 15).astype(F32)
    decoded = dec_ref[...].astype(BF16).reshape(FIELDS * ROWS, elems)

    def dispatch(base):
        cell = lax.broadcasted_iota(jnp.int32, (half * cap, elems), 0) + base * cap
        rows = lax.dot_general(
            (cell == slot).astype(F32).astype(BF16),
            decoded,
            (((1,), (1,)), ((), ())),
            preferred_element_type=F32,
        )
        rows = jnp.concatenate(
            [rows[:, f * ROWS : (f + 1) * ROWS].reshape(half, cap, ROWS) for f in range(FIELDS)],
            axis=1,
        )
        send_ref[pl.ds(base, half)] = rows.astype(BF16)

    def far(k):
        return far_base + lax.rem(me + k, half)

    def near(k):
        return my_base + lax.rem(me + k, half)

    def row_copy(other, landing):
        return pltpu.make_async_remote_copy(
            src_ref=send_ref.at[other],
            dst_ref=recv_ref.at[landing],
            send_sem=send_sem.at[other],
            recv_sem=recv_sem.at[landing],
            device_id=place_of(other),
            device_id_type=MESH,
        )

    def start_rows(k, carry):
        row_copy(lax.rem(me + k, devices), me).start()
        return carry

    dispatch(far_base)
    dispatch(my_base)
    pl.semaphore_wait(barrier, devices - 1)
    ahead = devices // 2
    lax.fori_loop(1, ahead, start_rows, 0)
    recv_ref[me] = send_ref[me]

    bulk = bulk_ref[...]
    inverse = 1.0 / rho_ref[...]

    def store_split(f, value):
        high, low = split(value)
        hl_ref[2 * f * ROWS : (2 * f + 1) * ROWS, :] = high
        hl_ref[(2 * f + 1) * ROWS : (2 * f + 2) * ROWS, :] = low

    def operator(gain):
        grad = dot(table_ref[0 : 3 * ROWS, :], hl_ref[0 : 2 * ROWS, :])
        diverge = sum(
            dot(
                table_ref[i * ROWS : (i + 1) * ROWS, :],
                hl_ref[2 * (i + 1) * ROWS : 2 * (i + 2) * ROWS, :],
            )
            for i in range(3)
        )
        by_bulk = bulk * (-gain / 3.0)
        by_rho = inverse * (-gain / 3.0)
        return [by_bulk * diverge] + [
            by_rho * grad[i * ROWS : (i + 1) * ROWS] for i in range(3)
        ]

    acc_ref[:, 0:NODES, :] = jnp.swapaxes(adj_ref[...], 0, 1)
    for f in range(FIELDS):
        acc_ref[f, NODES:ROWS, :] = jnp.zeros((ROWS - NODES, elems), F32)
    for f in range(FIELDS):
        store_split(f, acc_ref[f])
    for power in range(1, ORDER + 1):
        series = operator(time_step / (power + 1))
        for f in range(FIELDS):
            total = acc_ref[f] + series[f]
            acc_ref[f] = total
            store_split(f, total if power == ORDER else series[f])

    pick = table_ref[3 * ROWS : 3 * ROWS + 6 * FROWS, :]
    place = table_ref[3 * ROWS + 6 * FROWS :, :]
    traces = [dot(pick, hl_ref[2 * f * ROWS : (2 * f + 2) * ROWS, :]) for f in range(FIELDS)]
    half_bulk = 0.5 * bulk
    half_inverse = 0.5 * inverse
    for face in range(6):
        axis = face // 2
        sign = -1.0 if face % 2 == 0 else 1.0
        rows = [t[face * FROWS : (face + 1) * FROWS] for t in traces]
        flux_p = (sign * half_bulk) * rows[1 + axis]
        flux_v = (sign * half_inverse) * rows[0]
        for f in range(FIELDS):
            flux = flux_p if f == 0 else flux_v if f == 1 + axis else None
            given = rows[f] if flux is None else rows[f] + flux
            kept = rows[f] if flux is None else rows[f] - flux
            high, low = split(given)
            w_ref[face, f * FROWS : (f + 1) * FROWS, :] = high
            w_ref[face, ROWS + f * FROWS : ROWS + (f + 1) * FROWS, :] = low
            u_ref[face, f * FROWS : (f + 1) * FROWS, :] = kept

    rim_cell = lax.broadcasted_iota(jnp.int32, (rim, elems), 0)
    rim_hot = [
        (rim_cell + (elems + side * rim) == nb_ref[4 + side : 5 + side, :]).astype(F32).astype(BF16)
        for side in range(2)
    ]
    for side in range(2):
        rim_out[side] = lax.dot_general(
            w_ref[4 + side, 0:ROWS, :],
            rim_hot[side],
            (((1,), (1,)), ((), ())),
            preferred_element_type=F32,
        ).astype(BF16)

    def rim_copy(side, other):
        return pltpu.make_async_remote_copy(
            src_ref=rim_out.at[side],
            dst_ref=rim_in.at[1 - side],
            send_sem=rim_send_sem.at[side],
            recv_sem=rim_recv_sem.at[1 - side],
            device_id=place_of(other),
            device_id_type=MESH,
        )

    has_below = me > 0
    has_above = me < devices - 1

    @pl.when(has_below)
    def _():
        rim_copy(0, me - 1).start()

    @pl.when(has_above)
    def _():
        rim_copy(1, me + 1).start()

    lax.fori_loop(ahead, devices, start_rows, 0)

    @pl.when(me == 0)
    def _():
        rim_in[0] = jnp.zeros((ROWS, rim), BF16)

    @pl.when(me == devices - 1)
    def _():
        rim_in[1] = jnp.zeros((ROWS, rim), BF16)

    volume = operator(time_step)
    for f in range(FIELDS):
        sum_ref[f] = volume[f]

    cell = lax.broadcasted_iota(jnp.int32, (elems, elems), 0)
    for face in range(6):
        hot = (cell == nb_ref[face : face + 1, :]).astype(F32).astype(BF16)
        both = dot(w_ref[face ^ 1], hot)
        jump = both[0:ROWS] + both[ROWS:] - u_ref[face]
        for f in range(FIELDS):
            high, low = split(jump[f * FROWS : (f + 1) * FROWS])
            j_ref[f, face * FROWS : (face + 1) * FROWS, :] = high
            j_ref[f, (8 + face) * FROWS : (9 + face) * FROWS, :] = low
    for f in range(FIELDS):
        sum_ref[f] = sum_ref[f] + (time_step * lift_gain) * dot(
            place[:, 0 : 6 * FROWS], j_ref[f, 8 * FROWS : 14 * FROWS, :]
        )

    def scatter(base):
        arrived = recv_ref[pl.ds(base, half)].astype(F32)
        arrived = jnp.concatenate(
            [
                arrived[:, f * cap : (f + 1) * cap, :].reshape(half * cap, ROWS)
                for f in range(FIELDS)
            ],
            axis=1,
        )
        target = arrived[:, NODES : NODES + 1] * 16.0 + arrived[:, NODES + 1 : NODES + 2] - 1.0
        hot = (
            lax.broadcasted_iota(jnp.int32, (half * cap, elems), 1) == target.astype(jnp.int32)
        ).astype(F32)
        return lax.dot_general(
            arrived.astype(BF16),
            hot.astype(BF16),
            (((0,), (0,)), ((), ())),
            preferred_element_type=F32,
        )

    def wait_near(k, carry):
        other = near(k)
        row_copy(other, other).wait_recv()
        return carry

    def wait_far(k, carry):
        other = far(k)
        row_copy(other, other).wait_recv()
        return carry

    lax.fori_loop(1, half, wait_near, 0)
    dec_ref[...] = scatter(my_base).reshape(FIELDS, ROWS, elems)
    @pl.when(has_above)
    def _():
        rim_copy(0, me + 1).wait_recv()

    @pl.when(has_below)
    def _():
        rim_copy(1, me - 1).wait_recv()

    outer = [dot(rim_in[side], rim_hot[side]).astype(BF16) for side in range(2)]
    for f in range(FIELDS):
        for side in range(2):
            j_ref[f, (6 + side) * FROWS : (7 + side) * FROWS, :] = outer[side][
                f * FROWS : (f + 1) * FROWS
            ]
        sum_ref[f] = sum_ref[f] + (time_step * lift_gain) * dot(
            place, j_ref[f, 0 : 8 * FROWS, :]
        )
    upd_ref[...] = jnp.swapaxes(sum_ref[:, 0:NODES, :], 0, 1)

    lax.fori_loop(0, half, wait_far, 0)
    snapshot = scatter(far_base)
    product = [
        (snapshot[f * ROWS : (f + 1) * ROWS] + dec_ref[f]) * acc_ref[f] for f in range(FIELDS)
    ]
    image = jnp.stack([product[0], product[1] + product[2] + product[3]], axis=0)
    img_ref[...] = jnp.swapaxes(image[:, 0:NODES, :], 0, 1)

    def wait_sent(k, carry):
        other = lax.rem(me + k, devices)
        row_copy(other, me).wait_send()
        return carry

    lax.fori_loop(1, devices, wait_sent, 0)

    @pl.when(has_below)
    def _():
        rim_copy(0, me - 1).wait_send()

    @pl.when(has_above)
    def _():
        rim_copy(1, me + 1).wait_send()


def local(adjoint, bulk, density, neighbours, keyframe, codes, exponents, group_elem):
    elems = adjoint.shape[2]
    devices = lax.axis_size(("dom", "sub"))
    subs = lax.axis_size("sub")
    rim = GX * GY
    mean = elems // devices
    cap = -(-(mean + mean // 4) // 8) * 8
    packed = FIELDS * cap
    vmem = pl.BlockSpec(memory_space=pltpu.VMEM)
    shift = jnp.maximum(exponents[:, None, :], codes - 256) + 8
    delta = lax.shift_left(codes, shift)
    coded = (keyframe.astype(F32) + delta.astype(F32) * 2.0**-8).astype(BF16)
    update, image = pl.pallas_call(
        functools.partial(kernel, devices, subs, cap),
        out_shape=(
            jax.ShapeDtypeStruct((NODES, FIELDS, elems), F32),
            jax.ShapeDtypeStruct((NODES, 2, elems), F32),
        ),
        in_specs=[vmem] * 7,
        out_specs=(vmem, vmem),
        scratch_shapes=[
            pltpu.VMEM((FIELDS, ROWS, elems), F32),
            pltpu.VMEM((2 * FIELDS * ROWS, elems), BF16),
            pltpu.VMEM((FIELDS, ROWS, elems), F32),
            pltpu.VMEM((FIELDS, ROWS, elems), F32),
            pltpu.VMEM((6, 2 * ROWS, elems), BF16),
            pltpu.VMEM((6, ROWS, elems), F32),
            pltpu.VMEM((FIELDS, 14 * FROWS, elems), BF16),
            pltpu.VMEM((devices, packed, ROWS), BF16),
            pltpu.VMEM((devices, packed, ROWS), BF16),
            pltpu.VMEM((2, ROWS, rim), BF16),
            pltpu.VMEM((2, ROWS, rim), BF16),
            pltpu.SemaphoreType.DMA((devices,)),
            pltpu.SemaphoreType.DMA((devices,)),
            pltpu.SemaphoreType.DMA((2,)),
            pltpu.SemaphoreType.DMA((2,)),
        ],
        compiler_params=pltpu.CompilerParams(
            collective_id=0, has_side_effects=True, vmem_limit_bytes=40 * 1024 * 1024
        ),
    )(
        bulk.reshape(1, elems),
        density.reshape(1, elems),
        neighbours,
        group_elem.reshape(1, elems),
        jnp.swapaxes(coded, 0, 1),
        jnp.swapaxes(adjoint, 0, 1),
        tables(),
    )
    return jnp.swapaxes(update, 0, 1), jnp.swapaxes(image, 0, 1)


def solution(mesh):
    placed = (
        P(None, None, ("shot", "dom", "sub")),
        P(("shot", "dom", "sub")),
        P(("shot", "dom", "sub")),
        P(None, ("shot", "dom", "sub")),
        P(None, None, ("shot", "dom", "sub")),
        P(None, None, ("shot", "dom", "sub")),
        P(None, ("shot", "dom", "sub")),
        P(("shot", "dom", "sub")),
    )
    return jax.shard_map(
        local,
        mesh=mesh,
        in_specs=placed,
        out_specs=(P(None, None, ("shot", "dom", "sub")), P(None, None, ("shot", "dom", "sub"))),
        check_vma=False,
    )
```
